512 devices in a mesh: seq: 64 (over y, z), head: 8 (over x, core).
Axes of the slice: x: 4, y: 8, z: 8, core: 2. Of those that a mesh axis runs over, the one named last changes fastest.
Arguments:
- inputs: bfloat16 [8192, 16384], P('seq', 'head')
- b_proj: bfloat16 [8192, 1024], P('seq', 'head'), may hold values from -6 to 6
- c_proj: bfloat16 [8192, 1024], P('seq', 'head'), may hold values from -0.5 to 0.5
- log_decay: float32 [8192, 256], P('seq', 'head')
- skip: float32 [256], P('head'), may hold values from 0.5 to 2
- init_state: bfloat16 [256, 64, 128], P('head'), may hold values from -6 to 6
- norm_gain: float32 [16384], P('head'), may hold values from 0.5 to 1.5
Outputs:
- layer_output: bfloat16 [8192, 16384], P('seq', 'head')
The draws below stay inside these ranges and needn't reach their ends.
All inputs are finite; a program needn't handle non-finite values.
Results may differ from the reference program's by a relative error of at most 0.0047.
Values sent between devices are 32-bit elements; how exact they have to be, the bound alone decides.
No kernel may reach another device: no remote copies, remote signals or barrier semaphores. Data moves between devices by JAX's collectives and lax.ppermute only.
A program may use at most 192 MiB of HBM per device.

```python
import math
import jax
import jax.numpy as jnp
from jax import lax

RECURRENT_UNITS = 256
HEAD_DIM = 64
STATE = 128
GROUPS = 8
BLOCK = 64
TOK_DEV = 128
INPUT_WORDS = 8192


def head_law(key, slow_low, slow_high):
    parts = jax.random.split(key, 4)
    position = jnp.arange(RECURRENT_UNITS, dtype=jnp.float32) / (RECURRENT_UNITS - 1)
    chance = slow_low + (slow_high - slow_low) * position
    slower = jax.random.uniform(parts[0], (RECURRENT_UNITS,), jnp.float32) < chance
    slow_rate = jnp.exp(jax.random.uniform(parts[1], (RECURRENT_UNITS,), jnp.float32, jnp.log(0.1), jnp.log(0.5))) / INPUT_WORDS
    fast_rate = jnp.exp(jax.random.uniform(parts[2], (RECURRENT_UNITS,), jnp.float32, jnp.log(1.0 / 1000.0), jnp.log(1.0 / 30.0)))
    forgetting_speed = jnp.where(slower, slow_rate, fast_rate)
    strength = jnp.exp(jnp.log(3.0) * position) * jnp.exp(jax.random.uniform(parts[3], (RECURRENT_UNITS,), jnp.float32, 0.0, jnp.log(4.0)))
    return (forgetting_speed, strength)


def draw_log_decay(key, part):
    forgetting_speed, strength = head_law(key, 0.25, 0.75)
    key = jax.random.fold_in(key, 11)
    parts = jax.random.split(key, 4)
    approximate_guess = jax.random.uniform(parts[0], (INPUT_WORDS, RECURRENT_UNITS), jnp.float32, 0.5, 1.5)
    accelerator_factor = jnp.exp(jax.random.uniform(parts[1], (INPUT_WORDS // TOK_DEV, RECURRENT_UNITS), jnp.float32, jnp.log(0.5), jnp.log(2.0)))
    accelerator_factor = jnp.repeat(accelerator_factor, TOK_DEV, axis=0)
    offset_sequence = jax.random.randint(parts[2], (3,), 0, INPUT_WORDS)
    objective_numbers = jax.random.uniform(parts[3], (3, RECURRENT_UNITS), jnp.float32, 0.2, 0.35)
    word_ordinal = jnp.arange(INPUT_WORDS)
    clustered_sets = jnp.zeros((INPUT_WORDS, RECURRENT_UNITS), jnp.float32)
    for option_picker in range(3):
        clustered_sets = clustered_sets + jnp.where((word_ordinal == offset_sequence[option_picker])[:, None], jnp.log(1.0 - objective_numbers[option_picker])[None, :], 0.0)
    return (-forgetting_speed[None, :] * approximate_guess * accelerator_factor + clustered_sets).astype(jnp.float32)


def draw_inputs(key, part):
    forgetting_speed, strength = head_law(key, 0.25, 0.75)
    key = jax.random.fold_in(key, 12)
    parts = jax.random.split(key, 2)
    factor = jnp.sqrt(2.0 * forgetting_speed * strength)
    noise = jax.random.normal(parts[0], (INPUT_WORDS, RECURRENT_UNITS, HEAD_DIM), jnp.float32)
    loudness = jnp.exp(jax.random.uniform(parts[1], (INPUT_WORDS // TOK_DEV, RECURRENT_UNITS), jnp.float32, -2.5, 2.5))
    loudness = jnp.repeat(loudness, TOK_DEV, axis=0)
    scaled = noise * factor[None, :, None] * loudness[:, :, None]
    return scaled.reshape(INPUT_WORDS, RECURRENT_UNITS * HEAD_DIM).astype(jnp.bfloat16)


def steps_of(rng, dims, cuts, low, top_value):
    def one(dim, blocks):
        steps = jax.random.uniform(jax.random.fold_in(jax.random.fold_in(rng, 6), dim), (blocks,), jnp.float32, low / len(cuts), top_value / len(cuts))
        return jnp.repeat(jnp.exp(steps), dims[dim] // blocks).reshape((-1,) + (1,) * (len(dims) - dim - 1))

    gain = one(*cuts[0])
    for cut in cuts[1:]:
        gain = gain * one(*cut)
    return gain


def centred(rng, shape, deviation, bound, shards=(), kind=jnp.bfloat16):
    values = deviation * jax.random.normal(rng, shape, jnp.float32)
    if shards:
        values = values * steps_of(rng, shape, shards, -0.22, 0.18)
    return jnp.clip(values, -bound, bound).astype(kind)


def setup_inputs(seed: int = 0) -> dict:
    keys = jax.random.split(jax.random.key(seed), 8)
    inputs = draw_inputs(jax.random.fold_in(keys[7], 71), 0)
    b_proj = centred(keys[1], (INPUT_WORDS, GROUPS * STATE), 1.0, 6.0, ((0, 64), (1, 8)))
    c_proj = centred(keys[2], (INPUT_WORDS, GROUPS * STATE), STATE ** -0.5, 0.5, ((0, 64), (1, 8)))
    log_decay = draw_log_decay(jax.random.fold_in(keys[7], 71), 0)
    skip = jnp.clip(jnp.exp(math.log(2.0) - 1.3862944 * jax.random.uniform(keys[4], (RECURRENT_UNITS,), jnp.float32) ** steps_of(keys[4], (RECURRENT_UNITS,), ((0, 8),), -0.2, 0.2)), 0.5, 2.0)
    init_state = centred(keys[5], (RECURRENT_UNITS, HEAD_DIM, STATE), 1.0, 6.0, ((0, 8),))
    norm_gain = jnp.clip(1.0 + 0.1 * jax.random.normal(keys[6], (RECURRENT_UNITS * HEAD_DIM,), jnp.float32), 0.5, 1.5)
    return {"inputs": inputs, "b_proj": b_proj, "c_proj": c_proj, "log_decay": log_decay, "skip": skip, "init_state": init_state, "norm_gain": norm_gain}


epsilon = 1e-05

def reference(inputs, b_proj, c_proj, log_decay, skip, init_state, norm_gain):
    blocks = INPUT_WORDS // BLOCK
    per_group = RECURRENT_UNITS // GROUPS
    highest = lax.Precision.HIGHEST
    rows_i = lax.broadcasted_iota(jnp.int32, (BLOCK, BLOCK), 0)
    cols_j = lax.broadcasted_iota(jnp.int32, (BLOCK, BLOCK), 1)
    causal = rows_i >= cols_j

    def advance(running, element):
        values_b, keys_b, query_c, decay_log = element
        values = values_b.reshape(BLOCK, RECURRENT_UNITS, HEAD_DIM).astype(jnp.float32)
        keys_f = keys_b.reshape(BLOCK, GROUPS, STATE).astype(jnp.float32)
        query_f = query_c.reshape(BLOCK, GROUPS, STATE).astype(jnp.float32)
        cumulative = jnp.cumsum(decay_log, axis=0)
        cumulative_h = cumulative.T
        scores = jnp.repeat(jnp.einsum('ign,jgn->gij', query_f, keys_f, precision=highest), per_group, axis=0)
        spread_log = cumulative_h[:, :, None] - cumulative_h[:, None, :]
        weights = jnp.where(causal, jnp.exp(jnp.where(causal, spread_log, 0.0)), 0.0) * scores
        weights = lax.optimization_barrier(weights.astype(jnp.bfloat16)).astype(jnp.float32)
        inside = jnp.einsum('hij,jhp->ihp', weights, values, precision=highest)
        grouped = running.reshape(GROUPS, per_group, HEAD_DIM, STATE)
        outside = jnp.einsum('ign,gepn->igep', query_f, grouped, precision=highest).reshape(BLOCK, RECURRENT_UNITS, HEAD_DIM)
        outside = outside * jnp.exp(cumulative)[:, :, None]
        result = inside + outside + skip[None, :, None] * values
        to_end = jnp.exp(cumulative[-1:, :] - cumulative)
        carried = lax.optimization_barrier((values * to_end[:, :, None]).astype(jnp.bfloat16)).astype(jnp.float32)
        weighted = carried.reshape(BLOCK, GROUPS, per_group, HEAD_DIM)
        fresh_state = jnp.einsum('jgep,jgn->gepn', weighted, keys_f, precision=highest).reshape(RECURRENT_UNITS, HEAD_DIM, STATE)
        running = jnp.exp(cumulative[-1])[:, None, None] * running + fresh_state
        flattened = result.reshape(BLOCK, RECURRENT_UNITS * HEAD_DIM)
        factor = lax.rsqrt(lax.optimization_barrier(jnp.mean(flattened * flattened, axis=1)) + epsilon)
        return (running, (flattened * factor[:, None] * norm_gain[None, :]).astype(jnp.bfloat16))
    element_seq = (inputs.reshape(blocks, BLOCK, RECURRENT_UNITS * HEAD_DIM), b_proj.reshape(blocks, BLOCK, GROUPS * STATE), c_proj.reshape(blocks, BLOCK, GROUPS * STATE), log_decay.reshape(blocks, BLOCK, RECURRENT_UNITS))
    _, outputs = lax.scan(advance, init_state.astype(jnp.float32), element_seq)
    return outputs.reshape(INPUT_WORDS, RECURRENT_UNITS * HEAD_DIM)
```

```python
import jax
import jax.numpy as jnp
from jax import lax
from jax.experimental import pallas as pl
from jax.experimental.pallas import tpu as pltpu
from jax.sharding import PartitionSpec as P

RECURRENT_UNITS = 256
HEAD_DIM = 64
STATE = 128
BLOCK = 64
TOK = 128
PAIRS = 16
SEQ = 64
CUT = 4
ROWS = STATE // CUT
SENT = ROWS + 1
EPSILON = 1e-05
INTERPRET = False

F32, BF16 = jnp.float32, jnp.bfloat16
HIGHEST = lax.Precision.HIGHEST


def iotas(shape):
    return lax.broadcasted_iota(jnp.int32, shape, 0), lax.broadcasted_iota(jnp.int32, shape, 1)


def ones_where(condition):
    return jnp.where(condition, 1.0, 0.0).astype(F32)


def by_head(values, pair):
    rows = values.shape[0]
    lane = lax.broadcasted_iota(jnp.int32, (rows, 128), 1)
    left = jnp.broadcast_to(values[:, 2 * pair : 2 * pair + 1], (rows, 128))
    right = jnp.broadcast_to(values[:, 2 * pair + 1 : 2 * pair + 2], (rows, 128))
    return jnp.where(lane < HEAD_DIM, left, right)


def summed(decay_ref, mask):
    return jnp.dot(decay_ref[...], ones_where(mask), precision=HIGHEST, preferred_element_type=F32)


def states_kernel(x_ref, b_ref, decay_ref, out_ref):
    row, col = iotas((TOK, TOK))
    after = summed(decay_ref, row > col).T
    to_end = jnp.exp(after)
    total = summed(decay_ref, row >= 0).T[0:1]
    keys = b_ref[...].astype(F32).T.astype(BF16)
    for pair in range(PAIRS):
        lanes = slice(128 * pair, 128 * pair + 128)
        carried = (x_ref[:, lanes].astype(F32) * by_head(to_end, pair)).astype(BF16)
        state = jnp.dot(keys, carried, preferred_element_type=F32)
        total_row = by_head(total, pair)
        for cut in range(CUT):
            base = SENT * (CUT * pair + cut)
            out_ref[base : base + ROWS, :] = state[ROWS * cut : ROWS * cut + ROWS]
            out_ref[base + ROWS : base + SENT, :] = total_row


def scan_kernel(states_ref, init_ref, out_ref, first):
    me = lax.axis_index("seq")
    pair, cut = me // CUT, me % CUT
    start = init_ref[pl.ds(2 * pair, 2)].astype(F32).reshape(2 * HEAD_DIM, STATE)
    first[...] = start.T
    running = first[pl.ds(pl.multiple_of(ROWS * cut, ROWS), ROWS), :]
    for device in range(SEQ):
        base = SENT * device
        out_ref[ROWS * device : ROWS * device + ROWS, :] = running
        factor = jnp.exp(states_ref[base + ROWS : base + SENT, :])
        running = factor * running + states_ref[base : base + ROWS, :]


def output_kernel(x_ref, b_ref, c_ref, decay_ref, skip_ref, entry_ref, y_ref, squares_ref):
    row, col = iotas((TOK, TOK))
    same = (row // BLOCK) == (col // BLOCK)
    in_block_t = summed(decay_ref, same & (row <= col))
    second_t = jnp.where(col[:32] < BLOCK, -summed(decay_ref, (row > col) & (row < BLOCK)), in_block_t)
    in_block = in_block_t.T
    grown = jnp.exp(summed(decay_ref, row <= col).T)
    query, keys = c_ref[...], b_ref[...]
    scores = lax.dot_general(query, keys, (((1,), (1,)), ((), ())), preferred_element_type=F32)
    twice = jnp.concatenate([query, query], axis=1)
    row_h, col_h = iotas((BLOCK, TOK))
    left = col_h < HEAD_DIM
    top_mask = (col_h % BLOCK) <= row_h
    low_mask = col_h <= row_h + BLOCK
    top_scores = scores[:BLOCK, :BLOCK]
    top_scores = jnp.concatenate([top_scores, top_scores], axis=1)
    low_scores = scores[BLOCK:]
    skip = skip_ref[...]
    total = jnp.zeros((TOK, 128), F32)
    half_lane = lax.broadcasted_iota(jnp.int32, (TOK, 128), 1) < HEAD_DIM
    zero = jnp.zeros((TOK, 128), BF16)
    for pair in range(PAIRS):
        lanes = slice(128 * pair, 128 * pair + 128)
        h0, h1 = 2 * pair, 2 * pair + 1
        x = x_ref[:, lanes]
        x0 = jnp.where(half_lane, x, zero)
        x1 = jnp.where(half_lane, zero, x)
        top_row = jnp.concatenate([in_block_t[h0 : h0 + 1, :BLOCK], in_block_t[h1 : h1 + 1, :BLOCK]], axis=1)
        top = by_head(in_block[:BLOCK], pair) - top_row
        top = (jnp.exp(jnp.where(top_mask, top, -1e30)) * top_scores).astype(BF16)
        low = []
        for h in (h0, h1):
            spread = in_block[BLOCK:, h : h + 1] - second_t[h : h + 1, :]
            low.append((jnp.exp(jnp.where(low_mask, spread, -1e30)) * low_scores).astype(BF16))
        top_values = jnp.concatenate([x0[:BLOCK], x1[:BLOCK]], axis=0)
        inside_top = jnp.dot(top, top_values, preferred_element_type=F32)
        inside_low = jnp.dot(
            jnp.concatenate(low, axis=1), jnp.concatenate([x0, x1], axis=0), preferred_element_type=F32
        )
        inside = jnp.concatenate([inside_top, inside_low], axis=0)
        entry = entry_ref[128 * pair : 128 * pair + 128, :]
        high = entry.astype(BF16)
        rest = (entry - high.astype(F32)).astype(BF16)
        outside = jnp.dot(twice, jnp.concatenate([high, rest], axis=0), preferred_element_type=F32)
        y = inside + outside * by_head(grown, pair) + by_head(skip, pair) * x.astype(F32)
        y_ref[:, lanes] = y
        total = total + y * y
    squares_ref[...] = jnp.sum(total.T, axis=0, keepdims=True)


def norm_kernel(y_ref, squares_ref, gain_ref, out_ref):
    mean = jnp.sum(squares_ref[...], axis=0, keepdims=True) / (RECURRENT_UNITS * HEAD_DIM)
    factor = jnp.broadcast_to(lax.rsqrt(mean + EPSILON), (TOK, TOK)).T
    for pair in range(PAIRS):
        lanes = slice(128 * pair, 128 * pair + 128)
        out_ref[:, lanes] = (y_ref[:, lanes] * factor * gain_ref[:, lanes]).astype(BF16)


def call(kernel, outs, *args, scratch=()):
    return pl.pallas_call(
        kernel,
        out_shape=outs,
        scratch_shapes=scratch,
        interpret=INTERPRET,
        compiler_params=pltpu.CompilerParams(vmem_limit_bytes=32 * 1024 * 1024),
    )(*args)


def local(inputs, b_proj, c_proj, log_decay, skip, init_state, norm_gain):
    shape = jax.ShapeDtypeStruct
    decay = log_decay.T
    states = call(states_kernel, shape((SEQ * SENT, 128), F32), inputs, b_proj, decay)
    states = lax.all_to_all(states.reshape(SEQ, SENT, 1, 128), "seq", 0, 0, tiled=True)
    entries = call(
        scan_kernel,
        shape((SEQ * ROWS, 128), F32),
        states.reshape(SEQ * SENT, 128),
        init_state,
        scratch=[pltpu.VMEM((STATE, 128), F32)],
    )
    entries = lax.all_to_all(entries.reshape(SEQ, ROWS, 128), "seq", 0, 0, tiled=True)
    y, squares = call(
        output_kernel,
        (shape((TOK, PAIRS * 128), F32), shape((1, TOK), F32)),
        inputs,
        b_proj,
        c_proj,
        decay,
        skip.reshape(1, -1),
        entries.reshape(SEQ * ROWS, 128),
    )
    squares = lax.all_gather(squares, "head", axis=0, tiled=True)
    return call(norm_kernel, shape((TOK, PAIRS * 128), BF16), y, squares, norm_gain.reshape(1, -1))


def solution(mesh):
    in_specs = (
        P("seq", "head"),
        P("seq", "head"),
        P("seq", "head"),
        P("seq", "head"),
        P("head"),
        P("head", None, None),
        P("head"),
    )
    out_specs = P("seq", "head")
    return jax.shard_map(local, mesh=mesh, in_specs=in_specs, out_specs=out_specs, check_vma=False)
```

```python
import jax
import jax.numpy as jnp
from jax import lax
from jax.experimental import pallas as pl
from jax.experimental.pallas import tpu as pltpu
from jax.sharding import PartitionSpec as P

RECURRENT_UNITS = 256
HEAD_DIM = 64
STATE = 128
BLOCK = 64
TOK = 128
PAIRS = 16
SEQ = 64
CUT = 4
ROWS = STATE // CUT
SENT = ROWS + 1
PARTS = 2
WIDTH = PAIRS * 128 // PARTS
FIRST = [8 * ((SEQ - 1 - k) % 8) + (SEQ - 1 - k) // 8 for k in range(SEQ)]
SECOND = [SEQ - 1 - k for k in range(SEQ)]
EPSILON = 1e-05
INTERPRET = False

F32, BF16 = jnp.float32, jnp.bfloat16
HIGHEST = lax.Precision.HIGHEST


def iotas(shape):
    return lax.broadcasted_iota(jnp.int32, shape, 0), lax.broadcasted_iota(jnp.int32, shape, 1)


def ones_where(condition):
    return jnp.where(condition, 1.0, 0.0).astype(F32)


def by_head(values, pair):
    rows = values.shape[0]
    lane = lax.broadcasted_iota(jnp.int32, (rows, 128), 1)
    left = jnp.broadcast_to(values[:, 2 * pair : 2 * pair + 1], (rows, 128))
    right = jnp.broadcast_to(values[:, 2 * pair + 1 : 2 * pair + 2], (rows, 128))
    return jnp.where(lane < HEAD_DIM, left, right)


def summed(decay_ref, mask):
    return jnp.dot(decay_ref[...], ones_where(mask), precision=HIGHEST, preferred_element_type=F32)


def states_kernel(x_hbm, b_hbm, decay_hbm, out_hbm, x_ref, b_ref, decay_ref, out_ref, sems, out_sems):
    copies = [
        pltpu.make_async_copy(decay_hbm, decay_ref, sems.at[0]),
        pltpu.make_async_copy(b_hbm, b_ref, sems.at[1]),
    ]
    for part in range(PARTS):
        lanes = pl.ds(WIDTH * part, WIDTH)
        copies.append(
            pltpu.make_async_copy(x_hbm.at[:, lanes], x_ref.at[:, lanes], sems.at[2 + part])
        )
    for copy in copies:
        copy.start()
    row, col = iotas((TOK, TOK))
    copies[0].wait()
    after = summed(decay_ref, row > col).T
    to_end = jnp.exp(after)
    total = after[0:1] + decay_ref[...].T[0:1]
    copies[1].wait()
    keys = b_ref[...].astype(F32).T.astype(BF16)
    for pair in range(PAIRS):
        if pair % (PAIRS // PARTS) == 0:
            copies[2 + pair // (PAIRS // PARTS)].wait()
        lanes = slice(128 * pair, 128 * pair + 128)
        carried = (x_ref[:, lanes].astype(F32) * by_head(to_end, pair)).astype(BF16)
        state = jnp.dot(keys, carried, preferred_element_type=F32)
        total_row = by_head(total, pair)
        for cut in range(CUT):
            base = SENT * (CUT * pair + cut)
            out_ref[base : base + ROWS, :] = state[ROWS * cut : ROWS * cut + ROWS]
            out_ref[base + ROWS : base + SENT, :] = total_row
        if (pair + 1) % (PAIRS // PARTS) == 0:
            part = pair // (PAIRS // PARTS)
            rows = pl.ds(SEQ * SENT // PARTS * part, SEQ * SENT // PARTS)
            copies.append(
                pltpu.make_async_copy(out_ref.at[rows], out_hbm.at[rows], out_sems.at[part])
            )
            copies[-1].start()
    for copy in copies[2 + PARTS :]:
        copy.wait()


def scan_kernel(states_ref, first_ref, out_ref):
    running = first_ref[...]
    for device in range(SEQ):
        base = SENT * FIRST.index(device)
        place = ROWS * SECOND.index(device)
        out_ref[place : place + ROWS, :] = running
        factor = jnp.exp(states_ref[base + ROWS : base + SENT, :])
        running = factor * running + states_ref[base : base + ROWS, :]


def inside_kernel(
    x_ref, b_ref, c_ref, decay_ref, skip_ref, init_ref, inside_ref, grown_ref, first_ref, slice_ref
):
    me = lax.axis_index("seq")
    place = SEQ - 1 - (8 * (me % 8) + me // 8)
    start = init_ref[pl.ds(2 * (place // CUT), 2)].astype(F32).reshape(2 * HEAD_DIM, STATE)
    slice_ref[...] = start.T
    first_ref[...] = slice_ref[pl.ds(pl.multiple_of(ROWS * (place % CUT), ROWS), ROWS), :]
    row, col = iotas((TOK, TOK))
    same = (row // BLOCK) == (col // BLOCK)
    in_block_t = summed(decay_ref, same & (row <= col))
    second_t = jnp.where(col[:32] < BLOCK, -summed(decay_ref, (row > col) & (row < BLOCK)), in_block_t)
    in_block = in_block_t.T
    grown = jnp.exp(summed(decay_ref, row <= col).T)
    query, keys = c_ref[...], b_ref[...]
    scores = lax.dot_general(query, keys, (((1,), (1,)), ((), ())), preferred_element_type=F32)
    row_h, col_h = iotas((BLOCK, TOK))
    left = col_h < HEAD_DIM
    top_mask = (col_h % BLOCK) <= row_h
    low_mask = col_h <= row_h + BLOCK
    top_scores = scores[:BLOCK, :BLOCK]
    top_scores = jnp.concatenate([top_scores, top_scores], axis=1)
    low_scores = scores[BLOCK:]
    skip = skip_ref[...]
    half_lane = lax.broadcasted_iota(jnp.int32, (TOK, 128), 1) < HEAD_DIM
    zero = jnp.zeros((TOK, 128), BF16)
    for pair in range(PAIRS):
        lanes = slice(128 * pair, 128 * pair + 128)
        h0, h1 = 2 * pair, 2 * pair + 1
        x = x_ref[:, lanes]
        x0 = jnp.where(half_lane, x, zero)
        x1 = jnp.where(half_lane, zero, x)
        top_row = jnp.concatenate([in_block_t[h0 : h0 + 1, :BLOCK], in_block_t[h1 : h1 + 1, :BLOCK]], axis=1)
        top = by_head(in_block[:BLOCK], pair) - top_row
        top = (jnp.exp(jnp.where(top_mask, top, -1e30)) * top_scores).astype(BF16)
        low = []
        for h in (h0, h1):
            spread = in_block[BLOCK:, h : h + 1] - second_t[h : h + 1, :]
            low.append((jnp.exp(jnp.where(low_mask, spread, -1e30)) * low_scores).astype(BF16))
        top_values = jnp.concatenate([x0[:BLOCK], x1[:BLOCK]], axis=0)
        inside_top = jnp.dot(top, top_values, preferred_element_type=F32)
        inside_low = jnp.dot(
            jnp.concatenate(low, axis=1), jnp.concatenate([x0, x1], axis=0), preferred_element_type=F32
        )
        inside = jnp.concatenate([inside_top, inside_low], axis=0)
        grown_ref[:, lanes] = by_head(grown, pair)
        inside_ref[:, lanes] = inside + by_head(skip, pair) * x.astype(F32)


def output_kernel(c_ref, inside_ref, grown_ref, entry_ref, y_ref, squares_ref):
    query = c_ref[...]
    twice = jnp.concatenate([query, query], axis=1)
    total = jnp.zeros((TOK, 128), F32)
    for pair in range(PAIRS):
        lanes = slice(128 * pair, 128 * pair + 128)
        places = [ROWS * SECOND.index(FIRST[CUT * pair + cut]) for cut in range(CUT)]
        entry = jnp.concatenate([entry_ref[place : place + ROWS, :] for place in places], axis=0)
        high = entry.astype(BF16)
        rest = (entry - high.astype(F32)).astype(BF16)
        outside = jnp.dot(twice, jnp.concatenate([high, rest], axis=0), preferred_element_type=F32)
        y = inside_ref[:, lanes] + outside * grown_ref[:, lanes]
        y_ref[:, lanes] = y
        total = total + y * y
    squares_ref[...] = jnp.sum(total.T, axis=0, keepdims=True)


def norm_kernel(y_ref, squares_ref, gain_ref, out_hbm, out_ref, sems):
    mean = jnp.sum(squares_ref[...], axis=0, keepdims=True) / (RECURRENT_UNITS * HEAD_DIM)
    copies = []
    factor = jnp.broadcast_to(lax.rsqrt(mean + EPSILON), (TOK, TOK)).T
    for pair in range(PAIRS):
        lanes = slice(128 * pair, 128 * pair + 128)
        out_ref[:, lanes] = (y_ref[:, lanes] * factor * gain_ref[:, lanes]).astype(BF16)
        if (pair + 1) % (PAIRS // PARTS) == 0:
            part = pair // (PAIRS // PARTS)
            lanes = pl.ds(WIDTH * part, WIDTH)
            copies.append(
                pltpu.make_async_copy(out_ref.at[:, lanes], out_hbm.at[:, lanes], sems.at[part])
            )
            copies[-1].start()
    for copy in copies:
        copy.wait()


def call(kernel, outs, *args, **more):
    params = pltpu.CompilerParams(vmem_limit_bytes=32 * 1024 * 1024)
    return pl.pallas_call(kernel, out_shape=outs, interpret=INTERPRET, compiler_params=params, **more)(*args)


def in_hbm(value):
    return value if INTERPRET else pltpu.with_memory_space_constraint(value, pltpu.HBM)


def exchange(slices, order):
    return lax.all_to_all(slices, "seq", 0, 0, tiled=True, axis_index_groups=[order])


def local(inputs, b_proj, c_proj, log_decay, skip, init_state, norm_gain):
    shape = jax.ShapeDtypeStruct
    whole = shape((TOK, PAIRS * 128), F32)
    anywhere = pl.BlockSpec(memory_space=pl.ANY)
    decay = log_decay.T
    states = call(
        states_kernel,
        shape((SEQ * SENT, 128), F32),
        in_hbm(inputs),
        in_hbm(b_proj),
        in_hbm(decay),
        in_specs=[anywhere] * 3,
        out_specs=anywhere,
        scratch_shapes=[
            pltpu.VMEM(inputs.shape, BF16),
            pltpu.VMEM(b_proj.shape, BF16),
            pltpu.VMEM(decay.shape, F32),
            pltpu.VMEM((SEQ * SENT, 128), F32),
            pltpu.SemaphoreType.DMA((2 + PARTS,)),
            pltpu.SemaphoreType.DMA((PARTS,)),
        ],
    )
    states = exchange(states.reshape(SEQ, SENT, 1, 128), FIRST)
    inside, grown, first = call(
        inside_kernel,
        (whole, whole, shape((ROWS, 128), F32)),
        inputs,
        b_proj,
        c_proj,
        decay,
        skip.reshape(1, -1),
        init_state,
        scratch_shapes=[pltpu.VMEM((STATE, 128), F32)],
        cost_estimate=pl.CostEstimate(flops=1 << 31, bytes_accessed=1 << 24, transcendentals=1 << 20),
    )
    entries = call(
        scan_kernel,
        shape((SEQ * ROWS, 128), F32),
        states.reshape(SEQ * SENT, 128),
        first,
    )
    entries = exchange(entries.reshape(SEQ, ROWS, 128), SECOND)
    y, squares = call(
        output_kernel,
        (whole, shape((1, TOK), F32)),
        c_proj,
        inside,
        grown,
        entries.reshape(SEQ * ROWS, 128),
    )
    order = list(range(lax.axis_size("head")))[::-1]
    squares = lax.all_gather(squares, "head", axis=0, tiled=True, axis_index_groups=[order])
    return call(
        norm_kernel,
        shape((TOK, PAIRS * 128), BF16),
        y,
        squares,
        norm_gain.reshape(1, -1),
        out_specs=anywhere,
        scratch_shapes=[pltpu.VMEM((TOK, PAIRS * 128), BF16), pltpu.SemaphoreType.DMA((PARTS,))],
    )


def solution(mesh):
    in_specs = (
        P("seq", "head"),
        P("seq", "head"),
        P("seq", "head"),
        P("seq", "head"),
        P("head"),
        P("head", None, None),
        P("head"),
    )
    out_specs = P("seq", "head")
    return jax.shard_map(local, mesh=mesh, in_specs=in_specs, out_specs=out_specs, check_vma=False)
```

```python
import jax
import jax.numpy as jnp
from jax import lax
from jax.experimental import pallas as pl
from jax.experimental.pallas import tpu as pltpu
from jax.sharding import PartitionSpec as P

RECURRENT_UNITS = 256
HEAD_DIM = 64
STATE = 128
BLOCK = 64
TOK = 128
PAIRS = 16
SEQ = 64
CUT = 4
ROWS = STATE // CUT
SENT = ROWS + 1
PARTS = 2
WIDTH = PAIRS * 128 // PARTS
FIRST = [8 * ((SEQ - 1 - k) % 8) + (SEQ - 1 - k) // 8 for k in range(SEQ)]
SECOND = [SEQ - 1 - k for k in range(SEQ)]
HEADS = 8
EPSILON = 1e-05
INTERPRET = False

F32, BF16 = jnp.float32, jnp.bfloat16
HIGHEST = lax.Precision.HIGHEST


def iotas(shape):
    return lax.broadcasted_iota(jnp.int32, shape, 0), lax.broadcasted_iota(jnp.int32, shape, 1)


def ones_where(condition):
    return jnp.where(condition, 1.0, 0.0).astype(F32)


def by_head(values, pair):
    rows = values.shape[0]
    lane = lax.broadcasted_iota(jnp.int32, (rows, 128), 1)
    left = jnp.broadcast_to(values[:, 2 * pair : 2 * pair + 1], (rows, 128))
    right = jnp.broadcast_to(values[:, 2 * pair + 1 : 2 * pair + 2], (rows, 128))
    return jnp.where(lane < HEAD_DIM, left, right)


def summed(decay_ref, mask):
    return jnp.dot(decay_ref[...], ones_where(mask), precision=HIGHEST, preferred_element_type=F32)


def states_kernel(x_hbm, b_hbm, decay_hbm, out_hbm, x_ref, b_ref, decay_ref, out_ref, sems, out_sems):
    copies = [
        pltpu.make_async_copy(decay_hbm, decay_ref, sems.at[0]),
        pltpu.make_async_copy(b_hbm, b_ref, sems.at[1]),
    ]
    for part in range(PARTS):
        lanes = pl.ds(WIDTH * part, WIDTH)
        copies.append(
            pltpu.make_async_copy(x_hbm.at[:, lanes], x_ref.at[:, lanes], sems.at[2 + part])
        )
    for copy in copies:
        copy.start()
    row, col = iotas((TOK, TOK))
    copies[0].wait()
    after = summed(decay_ref, row > col).T
    to_end = jnp.exp(after)
    total = after[0:1] + decay_ref[...].T[0:1]
    copies[1].wait()
    keys = b_ref[...].astype(F32).T.astype(BF16)
    for pair in range(PAIRS):
        if pair % (PAIRS // PARTS) == 0:
            copies[2 + pair // (PAIRS // PARTS)].wait()
        lanes = slice(128 * pair, 128 * pair + 128)
        carried = (x_ref[:, lanes].astype(F32) * by_head(to_end, pair)).astype(BF16)
        state = jnp.dot(keys, carried, preferred_element_type=F32)
        total_row = by_head(total, pair)
        for cut in range(CUT):
            base = SENT * (CUT * pair + cut)
            out_ref[base : base + ROWS, :] = state[ROWS * cut : ROWS * cut + ROWS]
            out_ref[base + ROWS : base + SENT, :] = total_row
        if (pair + 1) % (PAIRS // PARTS) == 0:
            part = pair // (PAIRS // PARTS)
            rows = pl.ds(SEQ * SENT // PARTS * part, SEQ * SENT // PARTS)
            copies.append(
                pltpu.make_async_copy(out_ref.at[rows], out_hbm.at[rows], out_sems.at[part])
            )
            copies[-1].start()
    for copy in copies[2 + PARTS :]:
        copy.wait()


def scan_kernel(states_ref, first_ref, out_ref):
    running = first_ref[...]
    for device in range(SEQ):
        base = SENT * FIRST.index(device)
        place = ROWS * SECOND.index(device)
        out_ref[place : place + ROWS, :] = running
        factor = jnp.exp(states_ref[base + ROWS : base + SENT, :])
        running = factor * running + states_ref[base : base + ROWS, :]


def inside_kernel(
    x_ref, b_ref, c_ref, decay_ref, skip_ref, init_ref, inside_ref, grown_ref, first_ref, slice_ref
):
    me = lax.axis_index("seq")
    place = SEQ - 1 - (8 * (me % 8) + me // 8)
    start = init_ref[pl.ds(2 * (place // CUT), 2)].astype(F32).reshape(2 * HEAD_DIM, STATE)
    slice_ref[...] = start.T
    first_ref[...] = slice_ref[pl.ds(pl.multiple_of(ROWS * (place % CUT), ROWS), ROWS), :]
    row, col = iotas((TOK, TOK))
    same = (row // BLOCK) == (col // BLOCK)
    in_block_t = summed(decay_ref, same & (row <= col))
    second_t = jnp.where(col[:32] < BLOCK, -summed(decay_ref, (row > col) & (row < BLOCK)), in_block_t)
    in_block = in_block_t.T
    grown = jnp.exp(summed(decay_ref, row <= col).T)
    query, keys = c_ref[...], b_ref[...]
    scores = lax.dot_general(query, keys, (((1,), (1,)), ((), ())), preferred_element_type=F32)
    row_h, col_h = iotas((BLOCK, TOK))
    left = col_h < HEAD_DIM
    top_mask = (col_h % BLOCK) <= row_h
    low_mask = col_h <= row_h + BLOCK
    top_scores = scores[:BLOCK, :BLOCK]
    top_scores = jnp.concatenate([top_scores, top_scores], axis=1)
    low_scores = scores[BLOCK:]
    skip = skip_ref[...]
    half_lane = lax.broadcasted_iota(jnp.int32, (TOK, 128), 1) < HEAD_DIM
    zero = jnp.zeros((TOK, 128), BF16)
    for pair in range(PAIRS):
        lanes = slice(128 * pair, 128 * pair + 128)
        h0, h1 = 2 * pair, 2 * pair + 1
        x = x_ref[:, lanes]
        x0 = jnp.where(half_lane, x, zero)
        x1 = jnp.where(half_lane, zero, x)
        top_row = jnp.concatenate([in_block_t[h0 : h0 + 1, :BLOCK], in_block_t[h1 : h1 + 1, :BLOCK]], axis=1)
        top = by_head(in_block[:BLOCK], pair) - top_row
        top = (jnp.exp(jnp.where(top_mask, top, -1e30)) * top_scores).astype(BF16)
        low = []
        for h in (h0, h1):
            spread = in_block[BLOCK:, h : h + 1] - second_t[h : h + 1, :]
            low.append((jnp.exp(jnp.where(low_mask, spread, -1e30)) * low_scores).astype(BF16))
        top_values = jnp.concatenate([x0[:BLOCK], x1[:BLOCK]], axis=0)
        inside_top = jnp.dot(top, top_values, preferred_element_type=F32)
        inside_low = jnp.dot(
            jnp.concatenate(low, axis=1), jnp.concatenate([x0, x1], axis=0), preferred_element_type=F32
        )
        inside = jnp.concatenate([inside_top, inside_low], axis=0)
        grown_ref[:, lanes] = by_head(grown, pair)
        inside_ref[:, lanes] = inside + by_head(skip, pair) * x.astype(F32)


def output_kernel(c_ref, inside_ref, grown_ref, entry_ref, y_ref, squares_ref):
    query = c_ref[...]
    twice = jnp.concatenate([query, query], axis=1)
    total = jnp.zeros((TOK, 128), F32)
    for pair in range(PAIRS):
        lanes = slice(128 * pair, 128 * pair + 128)
        places = [ROWS * SECOND.index(FIRST[CUT * pair + cut]) for cut in range(CUT)]
        entry = jnp.concatenate([entry_ref[place : place + ROWS, :] for place in places], axis=0)
        high = entry.astype(BF16)
        rest = (entry - high.astype(F32)).astype(BF16)
        outside = jnp.dot(twice, jnp.concatenate([high, rest], axis=0), preferred_element_type=F32)
        y = inside_ref[:, lanes] + outside * grown_ref[:, lanes]
        y_ref[:, lanes] = y
        total = total + y * y
    squares_ref[...] = jnp.broadcast_to(jnp.sum(total.T, axis=0, keepdims=True), (HEADS, TOK))


def norm_kernel(y_ref, squares_ref, gain_ref, out_hbm, out_ref, sems):
    mean = jnp.sum(squares_ref[...], axis=0, keepdims=True) / (RECURRENT_UNITS * HEAD_DIM)
    copies = []
    factor = jnp.broadcast_to(lax.rsqrt(mean + EPSILON), (TOK, TOK)).T
    for pair in range(PAIRS):
        lanes = slice(128 * pair, 128 * pair + 128)
        out_ref[:, lanes] = (y_ref[:, lanes] * factor * gain_ref[:, lanes]).astype(BF16)
        if (pair + 1) % (PAIRS // PARTS) == 0:
            part = pair // (PAIRS // PARTS)
            lanes = pl.ds(WIDTH * part, WIDTH)
            copies.append(
                pltpu.make_async_copy(out_ref.at[:, lanes], out_hbm.at[:, lanes], sems.at[part])
            )
            copies[-1].start()
    for copy in copies:
        copy.wait()


def call(kernel, outs, *args, **more):
    params = pltpu.CompilerParams(vmem_limit_bytes=32 * 1024 * 1024)
    return pl.pallas_call(kernel, out_shape=outs, interpret=INTERPRET, compiler_params=params, **more)(*args)


def in_hbm(value):
    return value if INTERPRET else pltpu.with_memory_space_constraint(value, pltpu.HBM)


def exchange(slices, order):
    return lax.all_to_all(slices, "seq", 0, 0, tiled=True, axis_index_groups=[order])


def local(inputs, b_proj, c_proj, log_decay, skip, init_state, norm_gain):
    shape = jax.ShapeDtypeStruct
    whole = shape((TOK, PAIRS * 128), F32)
    anywhere = pl.BlockSpec(memory_space=pl.ANY)
    decay = log_decay.T
    states = call(
        states_kernel,
        shape((SEQ * SENT, 128), F32),
        in_hbm(inputs),
        in_hbm(b_proj),
        in_hbm(decay),
        in_specs=[anywhere] * 3,
        out_specs=anywhere,
        scratch_shapes=[
            pltpu.VMEM(inputs.shape, BF16),
            pltpu.VMEM(b_proj.shape, BF16),
            pltpu.VMEM(decay.shape, F32),
            pltpu.VMEM((SEQ * SENT, 128), F32),
            pltpu.SemaphoreType.DMA((2 + PARTS,)),
            pltpu.SemaphoreType.DMA((PARTS,)),
        ],
    )
    states = exchange(states.reshape(SEQ, SENT, 1, 128), FIRST)
    inside, grown, first = call(
        inside_kernel,
        (whole, whole, shape((ROWS, 128), F32)),
        inputs,
        b_proj,
        c_proj,
        decay,
        skip.reshape(1, -1),
        init_state,
        scratch_shapes=[pltpu.VMEM((STATE, 128), F32)],
        cost_estimate=pl.CostEstimate(flops=1 << 31, bytes_accessed=1 << 24, transcendentals=1 << 20),
    )
    entries = call(
        scan_kernel,
        shape((SEQ * ROWS, 128), F32),
        states.reshape(SEQ * SENT, 128),
        first,
    )
    entries = exchange(entries.reshape(SEQ, ROWS, 128), SECOND)
    y, squares = call(
        output_kernel,
        (whole, shape((HEADS, TOK), F32)),
        c_proj,
        inside,
        grown,
        entries.reshape(SEQ * ROWS, 128),
    )
    order = list(range(HEADS))[::-1]
    squares = lax.all_to_all(squares, "head", 0, 0, tiled=True, axis_index_groups=[order])
    return call(
        norm_kernel,
        shape((TOK, PAIRS * 128), BF16),
        y,
        squares,
        norm_gain.reshape(1, -1),
        out_specs=anywhere,
        scratch_shapes=[pltpu.VMEM((TOK, PAIRS * 128), BF16), pltpu.SemaphoreType.DMA((PARTS,))],
    )


def solution(mesh):
    in_specs = (
        P("seq", "head"),
        P("seq", "head"),
        P("seq", "head"),
        P("seq", "head"),
        P("head"),
        P("head", None, None),
        P("head"),
    )
    out_specs = P("seq", "head")
    return jax.shard_map(local, mesh=mesh, in_specs=in_specs, out_specs=out_specs, check_vma=False)
```

```python
import jax
import jax.numpy as jnp
from jax import lax
from jax.experimental import pallas as pl
from jax.experimental.pallas import tpu as pltpu
from jax.sharding import PartitionSpec as P

RECURRENT_UNITS = 256
HEAD_DIM = 64
STATE = 128
BLOCK = 64
TOK = 128
PAIRS = 16
SEQ = 64
CUT = 4
ROWS = STATE // CUT
SENT = ROWS + 1
PARTS = 2
WIDTH = PAIRS * 128 // PARTS
FIRST = [8 * ((SEQ - 1 - k) % 8) + (SEQ - 1 - k) // 8 for k in range(SEQ)]
SECOND = [SEQ - 1 - k for k in range(SEQ)]
HEADS = 8
EPSILON = 1e-05
INTERPRET = False

F32, BF16 = jnp.float32, jnp.bfloat16
HIGHEST = lax.Precision.HIGHEST


def iotas(shape):
    return lax.broadcasted_iota(jnp.int32, shape, 0), lax.broadcasted_iota(jnp.int32, shape, 1)


def ones_where(condition):
    return jnp.where(condition, 1.0, 0.0).astype(F32)


def by_head(values, pair):
    rows = values.shape[0]
    lane = lax.broadcasted_iota(jnp.int32, (rows, 128), 1)
    left = jnp.broadcast_to(values[:, 2 * pair : 2 * pair + 1], (rows, 128))
    right = jnp.broadcast_to(values[:, 2 * pair + 1 : 2 * pair + 2], (rows, 128))
    return jnp.where(lane < HEAD_DIM, left, right)


def summed(decay_ref, mask):
    return jnp.dot(decay_ref[...], ones_where(mask), precision=HIGHEST, preferred_element_type=F32)


def states_kernel(x_hbm, b_hbm, decay_hbm, out_hbm, x_ref, b_ref, decay_ref, out_ref, sems, out_sems):
    copies = [
        pltpu.make_async_copy(decay_hbm, decay_ref, sems.at[0]),
        pltpu.make_async_copy(b_hbm, b_ref, sems.at[1]),
    ]
    for part in range(PARTS):
        lanes = pl.ds(WIDTH * part, WIDTH)
        copies.append(
            pltpu.make_async_copy(x_hbm.at[:, lanes], x_ref.at[:, lanes], sems.at[2 + part])
        )
    for copy in copies:
        copy.start()
    row, col = iotas((TOK, TOK))
    copies[0].wait()
    after = summed(decay_ref, row > col).T
    to_end = jnp.exp(after)
    total = after[0:1] + decay_ref[...].T[0:1]
    copies[1].wait()
    keys = b_ref[...].astype(F32).T.astype(BF16)
    for pair in range(PAIRS):
        if pair % (PAIRS // PARTS) == 0:
            copies[2 + pair // (PAIRS // PARTS)].wait()
        lanes = slice(128 * pair, 128 * pair + 128)
        carried = (x_ref[:, lanes].astype(F32) * by_head(to_end, pair)).astype(BF16)
        state = jnp.dot(keys, carried, preferred_element_type=F32)
        total_row = by_head(total, pair)
        for cut in range(CUT):
            base = SENT * (CUT * pair + cut)
            out_ref[base : base + ROWS, :] = state[ROWS * cut : ROWS * cut + ROWS]
            out_ref[base + ROWS : base + SENT, :] = total_row
        if (pair + 1) % (PAIRS // PARTS) == 0:
            part = pair // (PAIRS // PARTS)
            rows = pl.ds(SEQ * SENT // PARTS * part, SEQ * SENT // PARTS)
            copies.append(
                pltpu.make_async_copy(out_ref.at[rows], out_hbm.at[rows], out_sems.at[part])
            )
            copies[-1].start()
    for copy in copies[2 + PARTS :]:
        copy.wait()


def scan_kernel(states_ref, first_ref, out_ref):
    running = first_ref[...]
    for device in range(SEQ):
        base = SENT * FIRST.index(device)
        place = ROWS * SECOND.index(device)
        out_ref[place : place + ROWS, :] = running
        factor = jnp.exp(states_ref[base + ROWS : base + SENT, :])
        running = factor * running + states_ref[base : base + ROWS, :]


def inside_kernel(
    x_ref, b_ref, c_ref, decay_ref, skip_ref, init_ref, inside_ref, grown_ref, first_ref, slice_ref
):
    me = lax.axis_index("seq")
    place = SEQ - 1 - (8 * (me % 8) + me // 8)
    start = init_ref[pl.ds(2 * (place // CUT), 2)].astype(F32).reshape(2 * HEAD_DIM, STATE)
    slice_ref[...] = start.T
    first_ref[...] = slice_ref[pl.ds(pl.multiple_of(ROWS * (place % CUT), ROWS), ROWS), :]
    row, col = iotas((TOK, TOK))
    same = (row // BLOCK) == (col // BLOCK)
    in_block_t = summed(decay_ref, same & (row <= col))
    second_t = jnp.where(col[:32] < BLOCK, -summed(decay_ref, (row > col) & (row < BLOCK)), in_block_t)
    in_block = in_block_t.T
    grown = jnp.exp(summed(decay_ref, row <= col).T)
    query, keys = c_ref[...], b_ref[...]
    scores = lax.dot_general(query, keys, (((1,), (1,)), ((), ())), preferred_element_type=F32)
    row_h, col_h = iotas((BLOCK, TOK))
    left = col_h < HEAD_DIM
    top_mask = (col_h % BLOCK) <= row_h
    low_mask = col_h <= row_h + BLOCK
    top_scores = scores[:BLOCK, :BLOCK]
    top_scores = jnp.concatenate([top_scores, top_scores], axis=1)
    low_scores = scores[BLOCK:]
    skip = skip_ref[...]
    half_lane = lax.broadcasted_iota(jnp.int32, (TOK, 128), 1) < HEAD_DIM
    zero = jnp.zeros((TOK, 128), BF16)
    for pair in range(PAIRS):
        lanes = slice(128 * pair, 128 * pair + 128)
        h0, h1 = 2 * pair, 2 * pair + 1
        x = x_ref[:, lanes]
        x0 = jnp.where(half_lane, x, zero)
        x1 = jnp.where(half_lane, zero, x)
        top_row = jnp.concatenate([in_block_t[h0 : h0 + 1, :BLOCK], in_block_t[h1 : h1 + 1, :BLOCK]], axis=1)
        top = by_head(in_block[:BLOCK], pair) - top_row
        top = (jnp.exp(jnp.where(top_mask, top, -1e30)) * top_scores).astype(BF16)
        low = []
        for h in (h0, h1):
            spread = in_block[BLOCK:, h : h + 1] - second_t[h : h + 1, :]
            low.append((jnp.exp(jnp.where(low_mask, spread, -1e30)) * low_scores).astype(BF16))
        top_values = jnp.concatenate([x0[:BLOCK], x1[:BLOCK]], axis=0)
        inside_top = jnp.dot(top, top_values, preferred_element_type=F32)
        inside_low = jnp.dot(
            jnp.concatenate(low, axis=1), jnp.concatenate([x0, x1], axis=0), preferred_element_type=F32
        )
        inside = jnp.concatenate([inside_top, inside_low], axis=0)
        grown_ref[:, lanes] = by_head(grown, pair)
        inside_ref[:, lanes] = inside + by_head(skip, pair) * x.astype(F32)


def output_kernel(c_ref, inside_ref, grown_ref, entry_ref, y_ref, squares_ref):
    query = c_ref[...]
    twice = jnp.concatenate([query, query], axis=1)
    total = jnp.zeros((TOK, 128), F32)
    for pair in range(PAIRS):
        lanes = slice(128 * pair, 128 * pair + 128)
        places = [ROWS * SECOND.index(FIRST[CUT * pair + cut]) for cut in range(CUT)]
        entry = jnp.concatenate([entry_ref[place : place + ROWS, :] for place in places], axis=0)
        high = entry.astype(BF16)
        rest = (entry - high.astype(F32)).astype(BF16)
        outside = jnp.dot(twice, jnp.concatenate([high, rest], axis=0), preferred_element_type=F32)
        y = inside_ref[:, lanes] + outside * grown_ref[:, lanes]
        y_ref[:, lanes] = y
        total = total + y * y
    squares_ref[...] = jnp.broadcast_to(jnp.sum(total.T, axis=0, keepdims=True), (HEADS, TOK))


def norm_kernel(y_ref, squares_ref, gain_ref, out_hbm, out_ref, sems):
    mean = jnp.sum(squares_ref[...], axis=0, keepdims=True) / (RECURRENT_UNITS * HEAD_DIM)
    copies = []
    factor = jnp.broadcast_to(lax.rsqrt(mean + EPSILON), (TOK, TOK)).T
    for pair in range(PAIRS):
        lanes = slice(128 * pair, 128 * pair + 128)
        out_ref[:, lanes] = (y_ref[:, lanes] * factor * gain_ref[:, lanes]).astype(BF16)
        if (pair + 1) % (PAIRS // PARTS) == 0:
            part = pair // (PAIRS // PARTS)
            lanes = pl.ds(WIDTH * part, WIDTH)
            copies.append(
                pltpu.make_async_copy(out_ref.at[:, lanes], out_hbm.at[:, lanes], sems.at[part])
            )
            copies[-1].start()
    for copy in copies:
        copy.wait()


def call(kernel, outs, *args, **more):
    params = pltpu.CompilerParams(vmem_limit_bytes=32 * 1024 * 1024)
    return pl.pallas_call(kernel, out_shape=outs, interpret=INTERPRET, compiler_params=params, **more)(*args)


def in_hbm(value):
    return value if INTERPRET else pltpu.with_memory_space_constraint(value, pltpu.HBM)


def exchange(slices, order):
    return lax.all_to_all(slices, "seq", 0, 0, tiled=True, axis_index_groups=[order])


def local(inputs, b_proj, c_proj, log_decay, skip, init_state, norm_gain):
    shape = jax.ShapeDtypeStruct
    whole = shape((TOK, PAIRS * 128), F32)
    anywhere = pl.BlockSpec(memory_space=pl.ANY)
    decay = log_decay.T
    states = call(
        states_kernel,
        shape((SEQ * SENT, 128), F32),
        in_hbm(inputs),
        in_hbm(b_proj),
        in_hbm(decay),
        in_specs=[anywhere] * 3,
        out_specs=anywhere,
        scratch_shapes=[
            pltpu.VMEM(inputs.shape, BF16),
            pltpu.VMEM(b_proj.shape, BF16),
            pltpu.VMEM(decay.shape, F32),
            pltpu.VMEM((SEQ * SENT, 128), F32),
            pltpu.SemaphoreType.DMA((2 + PARTS,)),
            pltpu.SemaphoreType.DMA((PARTS,)),
        ],
    )
    states = exchange(states.reshape(SEQ, SENT, 1, 128), FIRST)
    inside, grown, first = call(
        inside_kernel,
        (whole, whole, shape((ROWS, 128), F32)),
        inputs,
        b_proj,
        c_proj,
        decay,
        skip.reshape(1, -1),
        init_state,
        scratch_shapes=[pltpu.VMEM((STATE, 128), F32)],
        cost_estimate=pl.CostEstimate(flops=1 << 31, bytes_accessed=1 << 24, transcendentals=1 << 20),
    )
    entries = call(
        scan_kernel,
        shape((SEQ * ROWS, 128), F32),
        states.reshape(SEQ * SENT, 128),
        first,
    )
    entries = exchange(entries.reshape(SEQ, ROWS, 128), SECOND)
    y, squares = call(
        output_kernel,
        (whole, shape((HEADS, TOK), F32)),
        c_proj,
        inside,
        grown,
        entries.reshape(SEQ * ROWS, 128),
    )
    order = [(HEADS - 3 - k) % HEADS for k in range(HEADS)]
    squares = lax.all_to_all(squares, "head", 0, 0, tiled=True, axis_index_groups=[order])
    return call(
        norm_kernel,
        shape((TOK, PAIRS * 128), BF16),
        y,
        squares,
        norm_gain.reshape(1, -1),
        out_specs=anywhere,
        scratch_shapes=[pltpu.VMEM((TOK, PAIRS * 128), BF16), pltpu.SemaphoreType.DMA((PARTS,))],
    )


def solution(mesh):
    in_specs = (
        P("seq", "head"),
        P("seq", "head"),
        P("seq", "head"),
        P("seq", "head"),
        P("head"),
        P("head", None, None),
        P("head"),
    )
    out_specs = P("seq", "head")
    return jax.shard_map(local, mesh=mesh, in_specs=in_specs, out_specs=out_specs, check_vma=False)
```

```python
import jax
import jax.numpy as jnp
from jax import lax
from jax.experimental import pallas as pl
from jax.experimental.pallas import tpu as pltpu
from jax.sharding import PartitionSpec as P

RECURRENT_UNITS = 256
HEAD_DIM = 64
STATE = 128
BLOCK = 64
TOK = 128
PAIRS = 16
SEQ = 64
CUT = 4
ROWS = STATE // CUT
SENT = ROWS + 1
PARTS = 2
WIDTH = PAIRS * 128 // PARTS
FIRST = [8 * ((SEQ - 1 - k) % 8) + (SEQ - 1 - k) // 8 for k in range(SEQ)]
SECOND = [SEQ - 1 - k for k in range(SEQ)]
HEADS = 8
EPSILON = 1e-05
INTERPRET = False

F32, BF16 = jnp.float32, jnp.bfloat16
HIGHEST = lax.Precision.HIGHEST


def iotas(shape):
    return lax.broadcasted_iota(jnp.int32, shape, 0), lax.broadcasted_iota(jnp.int32, shape, 1)


def ones_where(condition):
    return jnp.where(condition, 1.0, 0.0).astype(F32)


def by_head(values, pair):
    rows = values.shape[0]
    lane = lax.broadcasted_iota(jnp.int32, (rows, 128), 1)
    left = jnp.broadcast_to(values[:, 2 * pair : 2 * pair + 1], (rows, 128))
    right = jnp.broadcast_to(values[:, 2 * pair + 1 : 2 * pair + 2], (rows, 128))
    return jnp.where(lane < HEAD_DIM, left, right)


def summed(decay_ref, mask):
    return jnp.dot(decay_ref[...], ones_where(mask), precision=HIGHEST, preferred_element_type=F32)


def states_kernel(x_hbm, b_hbm, decay_hbm, out_hbm, x_ref, b_ref, decay_ref, out_ref, sems, out_sems):
    copies = [
        pltpu.make_async_copy(decay_hbm, decay_ref, sems.at[0]),
        pltpu.make_async_copy(b_hbm, b_ref, sems.at[1]),
    ]
    copies.append(pltpu.make_async_copy(x_hbm, x_ref, sems.at[2]))
    for copy in copies:
        copy.start()
    row, col = iotas((TOK, TOK))
    copies[0].wait()
    after = summed(decay_ref, row > col)
    to_end = jnp.exp(after)
    total = (after + decay_ref[...]).T[0:1]
    copies[1].wait()
    keys = b_ref[...].astype(F32).T
    copies[2].wait()
    for pair in range(PAIRS):
        x = x_ref[:, 128 * pair : 128 * pair + 128]
        state = [
            jnp.dot((keys * to_end[h : h + 1]).astype(BF16), half, preferred_element_type=F32)
            for h, half in ((2 * pair, x[:, :HEAD_DIM]), (2 * pair + 1, x[:, HEAD_DIM:]))
        ]
        state = jnp.concatenate(state, axis=1)
        total_row = by_head(total, pair)
        for cut in range(CUT):
            base = SENT * (CUT * pair + cut)
            out_ref[base : base + ROWS, :] = state[ROWS * cut : ROWS * cut + ROWS]
            out_ref[base + ROWS : base + SENT, :] = total_row
        if (pair + 1) % (PAIRS // PARTS) == 0:
            part = pair // (PAIRS // PARTS)
            rows = pl.ds(SEQ * SENT // PARTS * part, SEQ * SENT // PARTS)
            copies.append(
                pltpu.make_async_copy(out_ref.at[rows], out_hbm.at[rows], out_sems.at[part])
            )
            copies[-1].start()
    for copy in copies[3:]:
        copy.wait()


def scan_kernel(states_ref, first_ref, out_ref):
    running = first_ref[...]
    for device in range(SEQ):
        base = SENT * FIRST.index(device)
        place = ROWS * SECOND.index(device)
        out_ref[place : place + ROWS, :] = running
        factor = jnp.exp(states_ref[base + ROWS : base + SENT, :])
        running = factor * running + states_ref[base : base + ROWS, :]


def inside_kernel(
    x_ref, b_ref, c_ref, decay_ref, skip_ref, init_ref, inside_ref, grown_ref, first_ref, slice_ref
):
    me = lax.axis_index("seq")
    place = SEQ - 1 - (8 * (me % 8) + me // 8)
    start = init_ref[pl.ds(2 * (place // CUT), 2)].astype(F32).reshape(2 * HEAD_DIM, STATE)
    slice_ref[...] = start.T
    first_ref[...] = slice_ref[pl.ds(pl.multiple_of(ROWS * (place % CUT), ROWS), ROWS), :]
    row, col = iotas((TOK, TOK))
    same = (row // BLOCK) == (col // BLOCK)
    in_block_t = summed(decay_ref, same & (row <= col))
    second_t = jnp.where(col[:32] < BLOCK, -summed(decay_ref, (row > col) & (row < BLOCK)), in_block_t)
    in_block = in_block_t.T
    grown = jnp.exp(summed(decay_ref, row <= col).T)
    query, keys = c_ref[...], b_ref[...]
    scores = lax.dot_general(query, keys, (((1,), (1,)), ((), ())), preferred_element_type=F32)
    row_h, col_h = iotas((BLOCK, TOK))
    left = col_h < HEAD_DIM
    top_mask = (col_h % BLOCK) <= row_h
    low_mask = col_h <= row_h + BLOCK
    top_scores = scores[:BLOCK, :BLOCK]
    top_scores = jnp.concatenate([top_scores, top_scores], axis=1)
    low_scores = scores[BLOCK:]
    skip = skip_ref[...]
    half_lane = lax.broadcasted_iota(jnp.int32, (TOK, 128), 1) < HEAD_DIM
    zero = jnp.zeros((TOK, 128), BF16)
    for pair in range(PAIRS):
        lanes = slice(128 * pair, 128 * pair + 128)
        h0, h1 = 2 * pair, 2 * pair + 1
        x = x_ref[:, lanes]
        x0 = jnp.where(half_lane, x, zero)
        x1 = jnp.where(half_lane, zero, x)
        top_row = jnp.concatenate([in_block_t[h0 : h0 + 1, :BLOCK], in_block_t[h1 : h1 + 1, :BLOCK]], axis=1)
        top = by_head(in_block[:BLOCK], pair) - top_row
        top = (jnp.exp(jnp.where(top_mask, top, -1e30)) * top_scores).astype(BF16)
        low = []
        for h in (h0, h1):
            spread = in_block[BLOCK:, h : h + 1] - second_t[h : h + 1, :]
            low.append((jnp.exp(jnp.where(low_mask, spread, -1e30)) * low_scores).astype(BF16))
        top_values = jnp.concatenate([x0[:BLOCK], x1[:BLOCK]], axis=0)
        inside_top = jnp.dot(top, top_values, preferred_element_type=F32)
        inside_low = jnp.dot(
            jnp.concatenate(low, axis=1), jnp.concatenate([x0, x1], axis=0), preferred_element_type=F32
        )
        inside = jnp.concatenate([inside_top, inside_low], axis=0)
        grown_ref[:, lanes] = by_head(grown, pair)
        inside_ref[:, lanes] = inside + by_head(skip, pair) * x.astype(F32)


def output_kernel(c_ref, inside_ref, grown_ref, entry_ref, y_ref, squares_ref):
    query = c_ref[...]
    twice = jnp.concatenate([query, query], axis=1)
    total = jnp.zeros((TOK, 128), F32)
    for pair in range(PAIRS):
        lanes = slice(128 * pair, 128 * pair + 128)
        places = [ROWS * SECOND.index(FIRST[CUT * pair + cut]) for cut in range(CUT)]
        entry = jnp.concatenate([entry_ref[place : place + ROWS, :] for place in places], axis=0)
        high = entry.astype(BF16)
        rest = (entry - high.astype(F32)).astype(BF16)
        outside = jnp.dot(twice, jnp.concatenate([high, rest], axis=0), preferred_element_type=F32)
        y = inside_ref[:, lanes] + outside * grown_ref[:, lanes]
        y_ref[:, lanes] = y
        total = total + y * y
    squares_ref[...] = jnp.broadcast_to(jnp.sum(total.T, axis=0, keepdims=True), (HEADS, TOK))


def norm_kernel(y_ref, squares_ref, gain_ref, out_hbm, out_ref, sems):
    mean = jnp.sum(squares_ref[...], axis=0, keepdims=True) / (RECURRENT_UNITS * HEAD_DIM)
    copies = []
    factor = jnp.broadcast_to(lax.rsqrt(mean + EPSILON), (TOK, TOK)).T
    for pair in range(PAIRS):
        lanes = slice(128 * pair, 128 * pair + 128)
        out_ref[:, lanes] = (y_ref[:, lanes] * factor * gain_ref[:, lanes]).astype(BF16)
        if (pair + 1) % (PAIRS // PARTS) == 0:
            part = pair // (PAIRS // PARTS)
            lanes = pl.ds(WIDTH * part, WIDTH)
            copies.append(
                pltpu.make_async_copy(out_ref.at[:, lanes], out_hbm.at[:, lanes], sems.at[part])
            )
            copies[-1].start()
    for copy in copies:
        copy.wait()


def call(kernel, outs, *args, **more):
    params = pltpu.CompilerParams(vmem_limit_bytes=32 * 1024 * 1024)
    return pl.pallas_call(kernel, out_shape=outs, interpret=INTERPRET, compiler_params=params, **more)(*args)


def in_hbm(value):
    return value if INTERPRET else pltpu.with_memory_space_constraint(value, pltpu.HBM)


def exchange(slices, order):
    return lax.all_to_all(slices, "seq", 0, 0, tiled=True, axis_index_groups=[order])


def local(inputs, b_proj, c_proj, log_decay, skip, init_state, norm_gain):
    shape = jax.ShapeDtypeStruct
    whole = shape((TOK, PAIRS * 128), F32)
    anywhere = pl.BlockSpec(memory_space=pl.ANY)
    decay = log_decay.T
    states = call(
        states_kernel,
        shape((SEQ * SENT, 128), F32),
        in_hbm(inputs),
        in_hbm(b_proj),
        in_hbm(decay),
        in_specs=[anywhere] * 3,
        out_specs=anywhere,
        scratch_shapes=[
            pltpu.VMEM(inputs.shape, BF16),
            pltpu.VMEM(b_proj.shape, BF16),
            pltpu.VMEM(decay.shape, F32),
            pltpu.VMEM((SEQ * SENT, 128), F32),
            pltpu.SemaphoreType.DMA((3,)),
            pltpu.SemaphoreType.DMA((PARTS,)),
        ],
    )
    states = exchange(states.reshape(SEQ, SENT, 1, 128), FIRST)
    inside, grown, first = call(
        inside_kernel,
        (whole, whole, shape((ROWS, 128), F32)),
        inputs,
        b_proj,
        c_proj,
        decay,
        skip.reshape(1, -1),
        init_state,
        scratch_shapes=[pltpu.VMEM((STATE, 128), F32)],
        cost_estimate=pl.CostEstimate(flops=1 << 31, bytes_accessed=1 << 24, transcendentals=1 << 20),
    )
    entries = call(
        scan_kernel,
        shape((SEQ * ROWS, 128), F32),
        states.reshape(SEQ * SENT, 128),
        first,
    )
    entries = exchange(entries.reshape(SEQ, ROWS, 128), SECOND)
    y, squares = call(
        output_kernel,
        (whole, shape((HEADS, TOK), F32)),
        c_proj,
        inside,
        grown,
        entries.reshape(SEQ * ROWS, 128),
    )
    order = [(HEADS - 3 - k) % HEADS for k in range(HEADS)]
    squares = lax.all_to_all(squares, "head", 0, 0, tiled=True, axis_index_groups=[order])
    return call(
        norm_kernel,
        shape((TOK, PAIRS * 128), BF16),
        y,
        squares,
        norm_gain.reshape(1, -1),
        out_specs=anywhere,
        scratch_shapes=[pltpu.VMEM((TOK, PAIRS * 128), BF16), pltpu.SemaphoreType.DMA((PARTS,))],
    )


def solution(mesh):
    in_specs = (
        P("seq", "head"),
        P("seq", "head"),
        P("seq", "head"),
        P("seq", "head"),
        P("head"),
        P("head", None, None),
        P("head"),
    )
    out_specs = P("seq", "head")
    return jax.shard_map(local, mesh=mesh, in_specs=in_specs, out_specs=out_specs, check_vma=False)
```

```python
import jax
import jax.numpy as jnp
from jax import lax
from jax.experimental import pallas as pl
from jax.experimental.pallas import tpu as pltpu
from jax.sharding import PartitionSpec as P

RECURRENT_UNITS = 256
HEAD_DIM = 64
STATE = 128
BLOCK = 64
TOK = 128
PAIRS = 16
SEQ = 64
CUT = 4
ROWS = STATE // CUT
SENT = ROWS + 1
PARTS = 2
WIDTH = PAIRS * 128 // PARTS
FIRST = [8 * ((SEQ - 1 - k) % 8) + (SEQ - 1 - k) // 8 for k in range(SEQ)]
SECOND = [SEQ - 1 - k for k in range(SEQ)]
HEADS = 8
EPSILON = 1e-05
INTERPRET = False

F32, BF16 = jnp.float32, jnp.bfloat16
HIGHEST = lax.Precision.HIGHEST


def iotas(shape):
    return lax.broadcasted_iota(jnp.int32, shape, 0), lax.broadcasted_iota(jnp.int32, shape, 1)


def ones_where(condition):
    return jnp.where(condition, 1.0, 0.0).astype(F32)


def by_head(values, pair):
    rows = values.shape[0]
    lane = lax.broadcasted_iota(jnp.int32, (rows, 128), 1)
    left = jnp.broadcast_to(values[:, 2 * pair : 2 * pair + 1], (rows, 128))
    right = jnp.broadcast_to(values[:, 2 * pair + 1 : 2 * pair + 2], (rows, 128))
    return jnp.where(lane < HEAD_DIM, left, right)


def summed(decay_ref, mask):
    return jnp.dot(decay_ref[...], ones_where(mask), precision=HIGHEST, preferred_element_type=F32)


def states_kernel(x_hbm, b_hbm, decay_hbm, out_hbm, x_ref, b_ref, decay_ref, out_ref, sems, out_sems):
    copies = [
        pltpu.make_async_copy(decay_hbm, decay_ref, sems.at[0]),
        pltpu.make_async_copy(b_hbm, b_ref, sems.at[1]),
    ]
    copies.append(pltpu.make_async_copy(x_hbm, x_ref, sems.at[2]))
    for copy in copies:
        copy.start()
    row, col = iotas((TOK, TOK))
    copies[0].wait()
    after = summed(decay_ref, row > col).T
    to_end = jnp.exp(after)
    total = after[0:1] + decay_ref[...].T[0:1]
    copies[1].wait()
    keys = b_ref[...].astype(F32).T.astype(BF16)
    copies[2].wait()
    for pair in range(PAIRS):
        lanes = slice(128 * pair, 128 * pair + 128)
        carried = (x_ref[:, lanes].astype(F32) * by_head(to_end, pair)).astype(BF16)
        state = jnp.dot(keys, carried, preferred_element_type=F32)
        total_row = by_head(total, pair)
        for cut in range(CUT):
            base = SENT * (CUT * pair + cut)
            out_ref[base : base + ROWS, :] = state[ROWS * cut : ROWS * cut + ROWS]
            out_ref[base + ROWS : base + SENT, :] = total_row
        if (pair + 1) % (PAIRS // PARTS) == 0:
            part = pair // (PAIRS // PARTS)
            rows = pl.ds(SEQ * SENT // PARTS * part, SEQ * SENT // PARTS)
            copies.append(
                pltpu.make_async_copy(out_ref.at[rows], out_hbm.at[rows], out_sems.at[part])
            )
            copies[-1].start()
    for copy in copies[3:]:
        copy.wait()


def scan_kernel(states_ref, first_ref, out_ref):
    running = first_ref[...]
    for device in range(SEQ):
        base = SENT * FIRST.index(device)
        place = ROWS * SECOND.index(device)
        out_ref[place : place + ROWS, :] = running
        factor = jnp.exp(states_ref[base + ROWS : base + SENT, :])
        running = factor * running + states_ref[base : base + ROWS, :]


def inside_kernel(
    x_ref, b_ref, c_ref, decay_ref, skip_ref, init_ref, inside_ref, grown_ref, first_ref, slice_ref
):
    me = lax.axis_index("seq")
    place = SEQ - 1 - (8 * (me % 8) + me // 8)
    start = init_ref[pl.ds(2 * (place // CUT), 2)].astype(F32).reshape(2 * HEAD_DIM, STATE)
    slice_ref[...] = start.T
    first_ref[...] = slice_ref[pl.ds(pl.multiple_of(ROWS * (place % CUT), ROWS), ROWS), :]
    row, col = iotas((TOK, TOK))
    same = (row // BLOCK) == (col // BLOCK)
    in_block_t = summed(decay_ref, same & (row <= col))
    second_t = jnp.where(col[:32] < BLOCK, -summed(decay_ref, (row > col) & (row < BLOCK)), in_block_t)
    in_block = in_block_t.T
    grown = jnp.exp(summed(decay_ref, row <= col).T)
    query, keys = c_ref[...], b_ref[...]
    scores = lax.dot_general(query, keys, (((1,), (1,)), ((), ())), preferred_element_type=F32)
    row_h, col_h = iotas((BLOCK, TOK))
    left = col_h < HEAD_DIM
    top_mask = (col_h % BLOCK) <= row_h
    low_mask = col_h <= row_h + BLOCK
    top_scores = scores[:BLOCK, :BLOCK]
    top_scores = jnp.concatenate([top_scores, top_scores], axis=1)
    low_scores = scores[BLOCK:]
    skip = skip_ref[...]
    half_lane = lax.broadcasted_iota(jnp.int32, (TOK, 128), 1) < HEAD_DIM
    zero = jnp.zeros((TOK, 128), BF16)
    for pair in range(PAIRS):
        lanes = slice(128 * pair, 128 * pair + 128)
        h0, h1 = 2 * pair, 2 * pair + 1
        x = x_ref[:, lanes]
        x0 = jnp.where(half_lane, x, zero)
        x1 = jnp.where(half_lane, zero, x)
        top_row = jnp.concatenate([in_block_t[h0 : h0 + 1, :BLOCK], in_block_t[h1 : h1 + 1, :BLOCK]], axis=1)
        top = by_head(in_block[:BLOCK], pair) - top_row
        top = (jnp.exp(jnp.where(top_mask, top, -1e30)) * top_scores).astype(BF16)
        low = []
        for h in (h0, h1):
            spread = in_block[BLOCK:, h : h + 1] - second_t[h : h + 1, :]
            low.append((jnp.exp(jnp.where(low_mask, spread, -1e30)) * low_scores).astype(BF16))
        top_values = jnp.concatenate([x0[:BLOCK], x1[:BLOCK]], axis=0)
        inside_top = jnp.dot(top, top_values, preferred_element_type=F32)
        inside_low = jnp.dot(
            jnp.concatenate(low, axis=1), jnp.concatenate([x0, x1], axis=0), preferred_element_type=F32
        )
        inside = jnp.concatenate([inside_top, inside_low], axis=0)
        grown_ref[:, lanes] = by_head(grown, pair)
        inside_ref[:, lanes] = inside + by_head(skip, pair) * x.astype(F32)


def output_kernel(c_ref, inside_ref, grown_ref, gain_ref, entry_ref, y_ref, squares_ref):
    query = c_ref[...]
    twice = jnp.concatenate([query, query], axis=1)
    total = jnp.zeros((TOK, 128), F32)
    for pair in range(PAIRS):
        lanes = slice(128 * pair, 128 * pair + 128)
        places = [ROWS * SECOND.index(FIRST[CUT * pair + cut]) for cut in range(CUT)]
        entry = jnp.concatenate([entry_ref[place : place + ROWS, :] for place in places], axis=0)
        high = entry.astype(BF16)
        rest = (entry - high.astype(F32)).astype(BF16)
        outside = jnp.dot(twice, jnp.concatenate([high, rest], axis=0), preferred_element_type=F32)
        y = inside_ref[:, lanes] + outside * grown_ref[:, lanes]
        y_ref[:, lanes] = y * gain_ref[:, lanes]
        total = total + y * y
    squares_ref[...] = jnp.broadcast_to(jnp.sum(total.T, axis=0, keepdims=True), (HEADS, TOK))


def norm_kernel(y_ref, squares_ref, out_hbm, out_ref, sems):
    mean = jnp.sum(squares_ref[...], axis=0, keepdims=True) / (RECURRENT_UNITS * HEAD_DIM)
    copies = []
    factor = jnp.broadcast_to(lax.rsqrt(mean + EPSILON), (TOK, TOK)).T
    for pair in range(PAIRS):
        lanes = slice(128 * pair, 128 * pair + 128)
        out_ref[:, lanes] = (y_ref[:, lanes] * factor).astype(BF16)
        if (pair + 1) % (PAIRS // PARTS) == 0:
            part = pair // (PAIRS // PARTS)
            lanes = pl.ds(WIDTH * part, WIDTH)
            copies.append(
                pltpu.make_async_copy(out_ref.at[:, lanes], out_hbm.at[:, lanes], sems.at[part])
            )
            copies[-1].start()
    for copy in copies:
        copy.wait()


def call(kernel, outs, *args, **more):
    params = pltpu.CompilerParams(vmem_limit_bytes=32 * 1024 * 1024)
    return pl.pallas_call(kernel, out_shape=outs, interpret=INTERPRET, compiler_params=params, **more)(*args)


def in_hbm(value):
    return value if INTERPRET else pltpu.with_memory_space_constraint(value, pltpu.HBM)


def exchange(slices, order):
    return lax.all_to_all(slices, "seq", 0, 0, tiled=True, axis_index_groups=[order])


def local(inputs, b_proj, c_proj, log_decay, skip, init_state, norm_gain):
    shape = jax.ShapeDtypeStruct
    whole = shape((TOK, PAIRS * 128), F32)
    anywhere = pl.BlockSpec(memory_space=pl.ANY)
    decay = log_decay.T
    states = call(
        states_kernel,
        shape((SEQ * SENT, 128), F32),
        in_hbm(inputs),
        in_hbm(b_proj),
        in_hbm(decay),
        in_specs=[anywhere] * 3,
        out_specs=anywhere,
        scratch_shapes=[
            pltpu.VMEM(inputs.shape, BF16),
            pltpu.VMEM(b_proj.shape, BF16),
            pltpu.VMEM(decay.shape, F32),
            pltpu.VMEM((SEQ * SENT, 128), F32),
            pltpu.SemaphoreType.DMA((3,)),
            pltpu.SemaphoreType.DMA((PARTS,)),
        ],
    )
    states = exchange(states.reshape(SEQ, SENT, 1, 128), FIRST)
    inside, grown, first = call(
        inside_kernel,
        (whole, whole, shape((ROWS, 128), F32)),
        inputs,
        b_proj,
        c_proj,
        decay,
        skip.reshape(1, -1),
        init_state,
        scratch_shapes=[pltpu.VMEM((STATE, 128), F32)],
        cost_estimate=pl.CostEstimate(flops=1 << 31, bytes_accessed=1 << 24, transcendentals=1 << 20),
    )
    entries = call(
        scan_kernel,
        shape((SEQ * ROWS, 128), F32),
        states.reshape(SEQ * SENT, 128),
        first,
    )
    entries = exchange(entries.reshape(SEQ, ROWS, 128), SECOND)
    y, squares = call(
        output_kernel,
        (whole, shape((HEADS, TOK), F32)),
        c_proj,
        inside,
        grown,
        norm_gain.reshape(1, -1),
        entries.reshape(SEQ * ROWS, 128),
    )
    order = [(HEADS - 3 - k) % HEADS for k in range(HEADS)]
    squares = lax.all_to_all(squares, "head", 0, 0, tiled=True, axis_index_groups=[order])
    return call(
        norm_kernel,
        shape((TOK, PAIRS * 128), BF16),
        y,
        squares,
        out_specs=anywhere,
        scratch_shapes=[pltpu.VMEM((TOK, PAIRS * 128), BF16), pltpu.SemaphoreType.DMA((PARTS,))],
    )


def solution(mesh):
    in_specs = (
        P("seq", "head"),
        P("seq", "head"),
        P("seq", "head"),
        P("seq", "head"),
        P("head"),
        P("head", None, None),
        P("head"),
    )
    out_specs = P("seq", "head")
    return jax.shard_map(local, mesh=mesh, in_specs=in_specs, out_specs=out_specs, check_vma=False)
```
